32 devices in a mesh: band: 2 (over y), strip: 4 (over z), src: 4 (over x, core).
Axes of the slice: x: 2, y: 2, z: 4, core: 2. Of those that a mesh axis runs over, the one named last changes fastest.
Arguments:
- theta: float32 [1024, 512], P(('band', 'strip')), parts along dimension 0, may hold values from -8 to 8
- target: int32 [1024, 512], P(('band', 'strip')), parts along dimension 0, may hold values 0 or 1
- source_shift: int32 [32, 2], P('src'), may hold values from -16 to 16
- source_weight: float32 [32], P('src'), may hold values from 0.14 to 7.1
Outputs:
- theta_final: float32 [1024, 512], P(('band', 'strip')), parts along dimension 0
- resist: float32 [1024, 512], P(('band', 'strip')), parts along dimension 0
The draws below stay inside these ranges and needn't reach their ends.
There are 2 independent parts, one for each index of `band`. The reference program is written for one: setup_inputs(seed, part) draws one part's arguments, and reference() takes and returns one part's arrays. A program takes and returns all parts, laid end to end along the dimension named above; an argument that names none is the same for every part. Nothing has to cross between parts.
All inputs are finite; a program needn't handle non-finite values. No bound on the sum of `target` on one device may be relied on, other than what follows from the above.
Results may differ from the reference program's by a relative error of at most 0.0055.
The reference program's roundings to bfloat16 on the way count: a program that leaves them out, or rounds other values in their place, can miss the bound.
Values may be sent and summed in bfloat16 or wider, within the bound.
A program may use at most 64 MiB of HBM per device.

```python
import math
import jax
import jax.numpy as jnp
from jax import lax

ROWS = 128
COLS = 512
HALO = 64
FREQ = 128
ITERS = 2
SOURCES = 32
NR = 512
N_STRIP = 4


def draw_source_weight(key, part):
    position = jnp.arange(SOURCES, dtype=jnp.float32) / max(SOURCES - 1, 1)
    jitter = jax.random.uniform(jax.random.fold_in(key, 7), (SOURCES,), jnp.float32, -0.0969, 0.0969)
    exponent = -0.5 + position
    return (10.0 ** (exponent + jitter)).astype(jnp.float32)


def touch_ends(drawn, own_key, least, largest):
    shape = drawn.shape
    place = [jax.random.randint(jax.random.fold_in(own_key, axis), (), 0, shape[axis]) for axis in range(len(shape))]
    drawn = drawn.at[tuple(place)].set(least)
    longest = shape.index(max(shape))
    place[longest] = (place[longest] + 1) % shape[longest]
    return drawn.at[tuple(place)].set(largest)


def shard_levels(rng, shape, shards, low, high):
    gain, own = 1.0, jax.random.fold_in(rng, 6)
    for dim, blocks in shards:
        steps = jnp.exp(jax.random.uniform(jax.random.fold_in(own, dim), (blocks,), jnp.float32, low / len(shards), high / len(shards)))
        gain = gain * jnp.repeat(steps, shape[dim] // blocks).reshape([-1 if axis == dim else 1 for axis in range(len(shape))])
    return gain


def bell_draw(own_key, dims, deviation, limit, shards=(), held_as=jnp.bfloat16):
    values = jax.random.normal(own_key, dims, jnp.float32) * deviation
    if len(shards) > 0:
        values = shard_levels(own_key, dims, shards, -0.22, 0.18) * values
    return jnp.clip(values, min=-limit, max=limit).astype(held_as)


def setup_inputs(seed: int = 0, part: int = 0) -> dict:
    key_of = jax.random.split(jax.random.key(seed), 5)
    part_splits = jax.random.split(jax.random.fold_in(key_of[4], part), 5)
    return {
        "theta": bell_draw(part_splits[0], (NR, COLS), 2.0, 8.0, ((0, 4),), jnp.float32),
        "target": touch_ends((jax.random.randint(part_splits[1], (NR, COLS), 0, 2) < 1).astype(jnp.int32), jax.random.fold_in(part_splits[1], 1), 0, 1),
        "source_shift": touch_ends(jax.random.randint(key_of[2], (SOURCES, 2), -(FREQ // 8), FREQ // 8 + 1), jax.random.fold_in(key_of[2], 1), -(FREQ // 8), (FREQ // 8 + 1) - 1).astype(jnp.int32),
        "source_weight": draw_source_weight(jax.random.fold_in(key_of[4], 71), part),
    }


steepness = 20.0
dose_level = 0.27
step_size = 1.0
epsilon = 1e-06

def phase_pair(freq_ids, points, period):
    index = freq_ids[:, None] % period * points[None, :] % period
    angle = 2.0 * math.pi / period * index.astype(jnp.float32)
    return (jnp.cos(angle), jnp.sin(angle))

def build_tables():
    freq_ids = jnp.arange(FREQ, dtype=jnp.int32) - FREQ // 2
    win_len = ROWS + 2 * HALO
    row_cos, row_sin = phase_pair(freq_ids, jnp.arange(win_len, dtype=jnp.int32), win_len)
    forward_rows = (jnp.concatenate([row_cos, -row_sin], 0) / win_len).astype(jnp.bfloat16)
    col_cos, col_sin = phase_pair(freq_ids, jnp.arange(COLS, dtype=jnp.int32), COLS)
    real_part = jnp.concatenate([col_cos.T, -col_sin.T], 1) / COLS
    imag_part = jnp.concatenate([col_sin.T, col_cos.T], 1) / COLS
    forward_cols = jnp.stack([real_part, imag_part], 0).astype(jnp.bfloat16)
    inverse_cols = jnp.concatenate([jnp.concatenate([col_cos, col_sin], 1), jnp.concatenate([-col_sin, col_cos], 1)], 0).astype(jnp.bfloat16)
    inner_cos, inner_sin = phase_pair(freq_ids, jnp.arange(ROWS, dtype=jnp.int32) + HALO, win_len)
    inner_cos, inner_sin = (inner_cos.T, inner_sin.T)
    inverse_rows = jnp.stack([jnp.stack([inner_cos, -inner_sin], 1), jnp.stack([inner_sin, inner_cos], 1)], 0).astype(jnp.bfloat16)
    return (forward_rows, forward_cols, inverse_cols, inverse_rows)

def pupil_of(shifts):
    grid = jnp.arange(FREQ, dtype=jnp.int32) - FREQ // 2
    along_k = grid[None, :] + shifts[:, 0:1]
    along_l = grid[None, :] + shifts[:, 1:2]
    radius = FREQ // 4
    inside = along_k[:, :, None] * along_k[:, :, None] + along_l[:, None, :] * along_l[:, None, :] <= radius * radius
    pupil = inside.astype(jnp.float32)
    return jnp.concatenate([pupil, pupil], 2).astype(jnp.bfloat16)

def imaging(window, pupil, weights, tables, total_sources):
    forward_rows, forward_cols, inverse_cols, inverse_rows = tables
    count = pupil.shape[0]
    half = jnp.dot(forward_rows, window, preferred_element_type=jnp.float32).astype(jnp.bfloat16)
    spectrum = jnp.einsum('pkc,pcl->kl', half.reshape(2, FREQ, COLS).astype(jnp.float32), forward_cols.astype(jnp.float32)).astype(jnp.bfloat16)
    passed = pupil * spectrum[None]
    columns = jnp.dot(passed.reshape(count * FREQ, 2 * FREQ), inverse_cols, preferred_element_type=jnp.float32).astype(jnp.bfloat16)
    columns = columns.reshape(count, FREQ, 2, COLS)
    field = jnp.einsum('pxqk,skqc->spxc', inverse_rows.astype(jnp.float32), columns.astype(jnp.float32))
    scaled = weights / total_sources
    partial_sum = lax.optimization_barrier(jnp.sum(scaled[:, None, None, None] * field * field, axis=(0, 1)))
    return (field, partial_sum)

def adjoint_spectrum(field, d_int, pupil, weights, tables, total_sources):
    forward_rows, forward_cols, inverse_cols, inverse_rows = tables
    count = pupil.shape[0]
    coeff = 2.0 * weights / total_sources
    d_field = (coeff[:, None, None, None] * d_int[None, None] * field).astype(jnp.bfloat16)
    d_columns = jnp.einsum('pxqk,spxc->skqc', inverse_rows.astype(jnp.float32), d_field.astype(jnp.float32)).astype(jnp.bfloat16)
    d_passed = jnp.dot(d_columns.reshape(count * FREQ, 2 * COLS), inverse_cols.T, preferred_element_type=jnp.float32)
    d_passed = d_passed.reshape(count, FREQ, 2 * FREQ)
    return lax.optimization_barrier(jnp.sum(d_passed * pupil.astype(jnp.float32), axis=0))

def adjoint_window(d_spectrum, tables):
    forward_rows, forward_cols, inverse_cols, inverse_rows = tables
    d_half = jnp.einsum('kl,pcl->pkc', d_spectrum, forward_cols.astype(jnp.float32), precision=lax.Precision.HIGHEST)
    d_half = d_half.reshape(2 * FREQ, COLS)
    return jnp.dot(forward_rows.astype(jnp.float32).T, d_half, precision=lax.Precision.HIGHEST)

def reference(theta, target, source_shift, source_weight):
    tables = build_tables()
    pupil = pupil_of(source_shift)
    win_len = ROWS + 2 * HALO
    target_strips = target.astype(jnp.float32).reshape(N_STRIP, ROWS, COLS)
    resist = jnp.zeros((NR, COLS), jnp.float32)
    for iteration in range(ITERS):
        mask_now = jax.nn.sigmoid(theta)
        mask_low = mask_now.astype(jnp.bfloat16)
        padded = jnp.concatenate([mask_low[NR - HALO:], mask_low, mask_low[:HALO]], 0)

        def one_strip(operands):
            strip_id, target_rows = operands
            window = lax.dynamic_slice_in_dim(padded, (strip_id * ROWS).astype(jnp.int32), win_len, 0)
            field, intensity = imaging(window, pupil, source_weight, tables, SOURCES)
            resist_rows = jax.nn.sigmoid(steepness * (intensity - dose_level))
            d_int = 2.0 * (resist_rows - target_rows) * steepness * resist_rows * (1.0 - resist_rows)
            d_spectrum = adjoint_spectrum(field, d_int, pupil, source_weight, tables, SOURCES)
            return (resist_rows, adjoint_window(d_spectrum, tables))
        resist_all, windows = lax.map(one_strip, (jnp.arange(N_STRIP, dtype=jnp.int32), target_strips))
        center = windows[:, HALO:HALO + ROWS]
        from_next = jnp.roll(windows[:, :HALO], -1, axis=0)
        from_prev = jnp.roll(windows[:, HALO + ROWS:], 1, axis=0)
        gradient = center.at[:, :HALO].add(from_prev)
        gradient = gradient.at[:, ROWS - HALO:].add(from_next).reshape(NR, COLS)
        d_theta = gradient * mask_now * (1.0 - mask_now)
        squares = jnp.sum(d_theta * d_theta)
        theta = theta - step_size * d_theta * lax.rsqrt(squares / (NR * COLS) + epsilon)
        resist = resist_all.reshape(NR, COLS)
    return (theta, resist)
```

```python
import functools
import math

import jax
import jax.numpy as jnp
import ml_dtypes
import numpy as np
from jax import lax
from jax.experimental import pallas as pl
from jax.experimental.pallas import tpu as pltpu
from jax.sharding import PartitionSpec as P

ROWS = 128
COLS = 512
HALO = 64
FREQ = 128
SRC_DEV = 8
ITERS = 2


steepness = 20.0
dose_level = 0.27
step_size = 1.0
epsilon = 1e-06


def extended(cells, sides, width):
    for axis, dim in sides:
        count = lax.axis_size(axis)
        head = lax.slice_in_dim(cells, 0, width, axis=dim)
        tail = lax.slice_in_dim(cells, cells.shape[dim] - width, cells.shape[dim], axis=dim)
        cells = jnp.concatenate(
            [
                lax.ppermute(tail, axis, [(i, (i + 1) % count) for i in range(count)]),
                cells,
                lax.ppermute(head, axis, [((i + 1) % count, i) for i in range(count)]),
            ],
            axis=dim,
        )
    return cells


def shifted(array, axis, by):
    size = lax.axis_size(axis)
    return lax.ppermute(array, axis, [(i, (i + by) % size) for i in range(size)])


def phase_pair(freq_ids, points, period):
    index = freq_ids[:, None] % period * points[None, :] % period
    angle = 2.0 * math.pi / period * index.astype(jnp.float32)
    return (jnp.cos(angle), jnp.sin(angle))


def build_tables():
    freq_ids = jnp.arange(FREQ, dtype=jnp.int32) - FREQ // 2
    win_len = ROWS + 2 * HALO
    row_cos, row_sin = phase_pair(freq_ids, jnp.arange(win_len, dtype=jnp.int32), win_len)
    forward_rows = (jnp.concatenate([row_cos, -row_sin], 0) / win_len).astype(jnp.bfloat16)
    col_cos, col_sin = phase_pair(freq_ids, jnp.arange(COLS, dtype=jnp.int32), COLS)
    real_part = jnp.concatenate([col_cos.T, -col_sin.T], 1) / COLS
    imag_part = jnp.concatenate([col_sin.T, col_cos.T], 1) / COLS
    forward_cols = jnp.stack([real_part, imag_part], 0).astype(jnp.bfloat16)
    inverse_cols = jnp.concatenate(
        [jnp.concatenate([col_cos, col_sin], 1), jnp.concatenate([-col_sin, col_cos], 1)], 0
    ).astype(jnp.bfloat16)
    inner_cos, inner_sin = phase_pair(freq_ids, jnp.arange(ROWS, dtype=jnp.int32) + HALO, win_len)
    inner_cos, inner_sin = (inner_cos.T, inner_sin.T)
    inverse_rows = jnp.stack(
        [jnp.stack([inner_cos, -inner_sin], 1), jnp.stack([inner_sin, inner_cos], 1)], 0
    ).astype(jnp.bfloat16)
    return (forward_rows, forward_cols, inverse_cols, inverse_rows)


def pupil_of(shifts):
    grid = jnp.arange(FREQ, dtype=jnp.int32) - FREQ // 2
    along_k = grid[None, :] + shifts[:, 0:1]
    along_l = grid[None, :] + shifts[:, 1:2]
    radius = FREQ // 4
    inside = (
        along_k[:, :, None] * along_k[:, :, None] + along_l[:, None, :] * along_l[:, None, :]
        <= radius * radius
    )
    pupil = inside.astype(jnp.float32)
    return jnp.concatenate([pupil, pupil], 2).astype(jnp.bfloat16)


def imaging(window, pupil, weights, tables, total_sources):
    forward_rows, forward_cols, inverse_cols, inverse_rows = tables
    count = pupil.shape[0]
    half = jnp.dot(forward_rows, window, preferred_element_type=jnp.float32).astype(jnp.bfloat16)
    spectrum = jnp.einsum(
        "pkc,pcl->kl", half.reshape(2, FREQ, COLS), forward_cols, preferred_element_type=jnp.float32
    ).astype(jnp.bfloat16)
    passed = pupil * spectrum[None]
    columns = jnp.dot(
        passed.reshape(count * FREQ, 2 * FREQ), inverse_cols, preferred_element_type=jnp.float32
    ).astype(jnp.bfloat16)
    columns = columns.reshape(count, FREQ, 2, COLS)
    field = jnp.einsum("pxqk,skqc->spxc", inverse_rows, columns, preferred_element_type=jnp.float32)
    scaled = weights / total_sources
    partial_sum = jnp.sum(scaled[:, None, None, None] * field * field, axis=(0, 1))
    return (field, partial_sum)


def adjoint_spectrum(field, d_int, pupil, weights, tables, total_sources):
    forward_rows, forward_cols, inverse_cols, inverse_rows = tables
    count = pupil.shape[0]
    coeff = 2.0 * weights / total_sources
    d_field = (coeff[:, None, None, None] * d_int[None, None] * field).astype(jnp.bfloat16)
    d_columns = jnp.einsum(
        "pxqk,spxc->skqc", inverse_rows, d_field, preferred_element_type=jnp.float32
    ).astype(jnp.bfloat16)
    d_passed = jnp.dot(
        d_columns.reshape(count * FREQ, 2 * COLS),
        inverse_cols.T,
        preferred_element_type=jnp.float32,
    )
    d_passed = d_passed.reshape(count, FREQ, 2 * FREQ)
    return jnp.sum(d_passed * pupil.astype(jnp.float32), axis=0)


def adjoint_window(d_spectrum, tables):
    forward_rows, forward_cols, inverse_cols, inverse_rows = tables
    d_half = jnp.einsum(
        "kl,pcl->pkc", d_spectrum, forward_cols.astype(jnp.float32), precision=lax.Precision.HIGHEST
    )
    d_half = d_half.reshape(2 * FREQ, COLS)
    return jnp.dot(forward_rows.astype(jnp.float32).T, d_half, precision=lax.Precision.HIGHEST)


def per_device(theta, target, source_shift, source_weight):
    tables = build_tables()
    pupil = pupil_of(source_shift)
    total_sources = SRC_DEV * lax.axis_size("src")
    total_cells = ROWS * lax.axis_size("strip") * COLS
    target_rows = target.astype(jnp.float32)
    resist = jnp.zeros((ROWS, COLS), jnp.float32)
    for iteration in range(ITERS):
        mask_now = jax.nn.sigmoid(theta)
        mask_low = mask_now.astype(jnp.bfloat16)
        window = extended(mask_low, (("strip", 0),), HALO)
        field, partial_sum = imaging(window, pupil, source_weight, tables, total_sources)
        intensity = lax.psum(partial_sum, "src")
        resist = jax.nn.sigmoid(steepness * (intensity - dose_level))
        d_int = 2.0 * (resist - target_rows) * steepness * resist * (1.0 - resist)
        d_spectrum = adjoint_spectrum(field, d_int, pupil, source_weight, tables, total_sources)
        d_window = adjoint_window(lax.psum(d_spectrum, "src"), tables)
        from_next = shifted(d_window[:HALO], "strip", -1)
        from_prev = shifted(d_window[HALO + ROWS :], "strip", 1)
        gradient = d_window[HALO : HALO + ROWS]
        gradient = gradient.at[:HALO].add(from_prev)
        gradient = gradient.at[ROWS - HALO :].add(from_next)
        d_theta = gradient * mask_now * (1.0 - mask_now)
        squares = lax.psum(jnp.sum(d_theta * d_theta), "strip")
        theta = theta - step_size * d_theta * lax.rsqrt(squares / total_cells + epsilon)
    return (theta, resist)


MESH = pl.DeviceIdType.MESH
LANES = 128
FIRST = FREQ // 2 - 3 * FREQ // 8
KEPT = FREQ - FIRST
WIN = ROWS + 2 * HALO
STEP = 8


def host_tables():
    freq = np.arange(FREQ) - FREQ // 2

    def pair(ids, points, period):
        angle = 2.0 * np.pi / period * (ids[:, None] % period * points[None, :] % period)
        return np.cos(angle).astype(np.float32), np.sin(angle).astype(np.float32)

    kept = freq[FIRST:]
    rc, rs = pair(kept, np.arange(WIN), WIN)
    rows = np.concatenate([rc, -rs], 0) / WIN
    cc, cs = pair(freq, np.arange(COLS), COLS)
    gc = np.concatenate([cc, -cs], 0)
    gs = np.concatenate([cs, cc], 0)
    ic, si = pair(kept, np.arange(ROWS) + HALO, WIN)
    inv = np.block([[ic.T, -si.T], [si.T, ic.T]])
    return [a.astype(ml_dtypes.bfloat16) for a in (rows, rows.T.copy(), gc, gs, inv, inv.T.copy())]


def dot(a, b):
    return jnp.dot(a, b, preferred_element_type=jnp.float32)


def dot_t(a, b):
    return lax.dot_general(a, b, (((1,), (1,)), ((), ())), preferred_element_type=jnp.float32)


def split2(a):
    high = a.astype(jnp.bfloat16)
    return high, (a - high.astype(jnp.float32)).astype(jnp.bfloat16)


def kernel(
    n_src, n_strip,
    shift_ref, weight_ref, theta_ref, target_ref,
    fr_ref, frt_ref, gc_ref, gs_ref, inv_ref, invt_ref,
    out_theta, out_resist,
    thw, mask_own, mask_top, mask_bot, pk, pupil, field, dsp, rs_in, gath, gbuf, res,
    pk_s, pk_r, halo_s, halo_r, rs_s, rs_r, z_s, z_r, ag_s, ag_r, g_s, g_r, res_s, res_r,
):
    me = lax.axis_index("src")
    strip = lax.axis_index("strip")
    total = n_src * SRC_DEV
    src_peers = [lax.rem(me + d, n_src) for d in range(1, n_src)]
    strip_peers = [lax.rem(strip + d, n_strip) for d in range(1, n_strip)]
    nxt, prv = strip_peers[0], strip_peers[-1]

    def send(here, there, ssem, rsem, **to):
        copy = pltpu.make_async_remote_copy(
            src_ref=here, dst_ref=there, send_sem=ssem, recv_sem=rsem, device_id=to, device_id_type=MESH
        )
        copy.start()
        pending.append(copy)
        return copy

    pending = []
    barrier = pltpu.get_barrier_semaphore()
    for p in src_peers:
        pl.semaphore_signal(barrier, inc=1, device_id={"src": p}, device_id_type=MESH)
    for p in strip_peers:
        pl.semaphore_signal(barrier, inc=1, device_id={"strip": p}, device_id_type=MESH)

    for i in range(SRC_DEV):
        pk[me, 0, i : i + 1, :] = jnp.full((1, LANES), shift_ref[i, 0].astype(jnp.float32))
        pk[me, 1, i : i + 1, :] = jnp.full((1, LANES), shift_ref[i, 1].astype(jnp.float32))
        pk[me, 2, i : i + 1, :] = jnp.full((1, LANES), weight_ref[i] / total)
    mask_own[...] = jax.nn.sigmoid(theta_ref[...]).astype(jnp.bfloat16)
    thw[HALO : HALO + ROWS, :] = theta_ref[...]
    pl.semaphore_wait(barrier, n_src - 1 + n_strip - 1)

    down = send(mask_own.at[ROWS - HALO :], mask_top, halo_s.at[0], halo_r.at[0], strip=nxt)
    up = send(mask_own.at[:HALO], mask_bot, halo_s.at[1], halo_r.at[1], strip=prv)
    packs = [send(pk.at[me], pk.at[me], pk_s.at[d], pk_r.at[d], src=p) for d, p in enumerate(src_peers)]
    th_down = send(theta_ref.at[ROWS - HALO :], thw.at[:HALO], halo_s.at[2], halo_r.at[2], strip=nxt)
    th_up = send(theta_ref.at[:HALO], thw.at[HALO + ROWS :], halo_s.at[3], halo_r.at[3], strip=prv)

    col = pl.ds(pl.multiple_of(me * LANES, LANES), LANES)
    g_mine = jnp.concatenate([gc_ref[:, col], gs_ref[:, col]], 1)
    target_mine = target_ref[:, col].astype(jnp.float32)

    for c in packs:
        c.wait_recv()

    k_id = lax.broadcasted_iota(jnp.int32, (KEPT, LANES), 0) + (FIRST - FREQ // 2)
    l_id = lax.broadcasted_iota(jnp.int32, (KEPT, LANES), 1) - FREQ // 2
    k_id, l_id = k_id.astype(jnp.float32), l_id.astype(jnp.float32)
    radius = float((FREQ // 4) ** 2)

    def make_pupil(s, carry):
        q, i = s // SRC_DEV, s % SRC_DEV
        a = k_id + pk[q, 0, pl.ds(i, 1), :]
        b = l_id + pk[q, 1, pl.ds(i, 1), :]
        pupil[s] = jnp.where(a * a + b * b <= radius, 1.0, 0.0).astype(jnp.bfloat16)
        return carry

    lax.fori_loop(0, total, make_pupil, 0)
    down.wait_recv()
    up.wait_recv()

    for it in range(ITERS):
        last = it == ITERS - 1
        if it == 0:
            window = jnp.concatenate([mask_top[...], mask_own[...], mask_bot[...]], 0)
        else:
            window = jax.nn.sigmoid(thw[...]).astype(jnp.bfloat16)
        half = dot(fr_ref[...], window).astype(jnp.bfloat16)
        spectrum = dot_t(half[:KEPT], gc_ref[...]) + dot_t(half[KEPT:], gs_ref[...])
        spectrum = (spectrum / COLS).astype(jnp.bfloat16)

        def forward(step, acc):
            inv = inv_ref[...]
            for pair in range(STEP // 2):
                stacked = []
                for j in range(2):
                    p = pupil[step * STEP + 2 * pair + j]
                    passed = spectrum * jnp.concatenate([p, p], 1)
                    cols = dot(passed, g_mine).astype(jnp.bfloat16)
                    stacked.append(jnp.concatenate([cols[:, :LANES], cols[:, LANES:]], 0))
                f = dot(inv, jnp.concatenate(stacked, 1))
                field[step * (STEP // 2) + pair] = f
                f2 = f * f
                for j in range(2):
                    w = pk[step, 2, 2 * pair + j : 2 * pair + j + 1, :]
                    part = f2[:, j * LANES : (j + 1) * LANES]
                    acc = acc + w * (part[:ROWS] + part[ROWS:])
            return acc

        intensity = lax.fori_loop(0, total // STEP, forward, jnp.zeros((ROWS, LANES), jnp.float32))
        resist = jax.nn.sigmoid(steepness * (intensity - dose_level))
        if last:
            res[me] = resist
            res_copies = [
                send(res.at[me], res.at[me], res_s.at[d], res_r.at[d], src=p)
                for d, p in enumerate(src_peers)
            ]
        d_int = 2.0 * (resist - target_mine) * steepness * resist * (1.0 - resist)

        def backward(step, acc):
            invt = invt_ref[...]
            for pair in range(STEP // 2):
                f = field[step * (STEP // 2) + pair]
                scaled = []
                for j in range(2):
                    w = 2.0 * pk[step, 2, 2 * pair + j : 2 * pair + j + 1, :]
                    d = w * d_int
                    scaled.append(jnp.concatenate([d, d], 0) * f[:, j * LANES : (j + 1) * LANES])
                d_field = jnp.concatenate(scaled, 1).astype(jnp.bfloat16)
                d_cols = dot(invt, d_field).astype(jnp.bfloat16)
                for j in range(2):
                    mine = d_cols[:, j * LANES : (j + 1) * LANES]
                    flat = jnp.concatenate([mine[:KEPT], mine[KEPT:]], 1)
                    p = pupil[step * STEP + 2 * pair + j].astype(jnp.float32)
                    acc = acc + jnp.concatenate([p, p], 1) * dot_t(flat, g_mine)
            return acc

        d_spec = lax.fori_loop(0, total // STEP, backward, jnp.zeros((KEPT, 2 * LANES), jnp.float32))
        part = KEPT // 2
        for q in range(n_src):
            r, c = q // 2, q % 2
            dsp[it, q] = d_spec[r * part : (r + 1) * part, c * LANES : (c + 1) * LANES]
        scatter = [
            send(dsp.at[it, p], rs_in.at[it, d], rs_s.at[it, d], rs_r.at[it, d], src=p)
            for d, p in enumerate(src_peers)
        ]
        mine = dsp[it, me]
        for d, c in enumerate(scatter):
            c.wait_recv()
            mine = mine + rs_in[it, d]
        gath[it, 0, me] = mine
        z_next = send(gath.at[it, 0, me], gath.at[it, 1, me], z_s.at[it, 0], z_r.at[it, 0], strip=nxt)
        z_prev = send(gath.at[it, 0, me], gath.at[it, 2, me], z_s.at[it, 1], z_r.at[it, 1], strip=prv)

        def share(rel):
            return [
                send(gath.at[it, rel, me], gath.at[it, rel, me], ag_s.at[it, rel, d], ag_r.at[it, rel, d], src=p)
                for d, p in enumerate(src_peers)
            ]

        shares = share(0)
        z_next.wait_recv()
        shares = shares + share(1)
        z_prev.wait_recv()
        shares = shares + share(2)

        def d_half(rel):
            full = jnp.concatenate(
                [jnp.concatenate([gath[it, rel, 0], gath[it, rel, 1]], 1),
                 jnp.concatenate([gath[it, rel, 2], gath[it, rel, 3]], 1)], 0)
            high, low = split2(full / COLS)
            both = jnp.concatenate([high, low], 0)
            out = []
            for g in (gc_ref, gs_ref):
                o = dot(both, g[...])
                out.append(o[:KEPT] + o[KEPT:])
            return split2(jnp.concatenate(out, 0))

        def back_rows(lo, hi, parts):
            t = frt_ref[lo:hi, :]
            return dot(t, parts[0]) + dot(t, parts[1])

        for c in shares[: n_src - 1]:
            c.wait_recv()
        own = d_half(0)
        center = back_rows(HALO, HALO + ROWS, own) if last else back_rows(0, WIN, own)
        for c in shares[n_src - 1 : 2 * (n_src - 1)]:
            c.wait_recv()
        prev = d_half(1)
        top = back_rows(HALO + ROWS if last else ROWS, WIN, prev)
        for c in shares[2 * (n_src - 1) :]:
            c.wait_recv()
        after = d_half(2)
        bottom = back_rows(0, HALO if last else WIN - ROWS, after)
        gradient = center + jnp.concatenate([top, bottom], 0)
        if it == 0:
            th_down.wait_recv()
            th_up.wait_recv()
        theta_now = thw[HALO : HALO + ROWS, :] if last else thw[...]
        m = jax.nn.sigmoid(theta_now)
        d_theta = gradient * m * (1.0 - m)
        inner = d_theta if last else d_theta[HALO : HALO + ROWS]
        sq = inner * inner
        sq = jnp.sum(sq.reshape(ROWS // 8, 8, COLS), axis=0)
        tile = sq[:, :LANES]
        for c in range(1, COLS // LANES):
            tile = tile + sq[:, c * LANES : (c + 1) * LANES]
        gbuf[it, strip] = tile
        norms = [
            send(gbuf.at[it, strip], gbuf.at[it, strip], g_s.at[it, d], g_r.at[it, d], strip=p)
            for d, p in enumerate(strip_peers)
        ]
        for c in norms:
            c.wait_recv()
        squares = jnp.sum(gbuf[it], axis=0)
        squares = jnp.sum(jnp.sum(squares, axis=1, keepdims=True), axis=0, keepdims=True)
        scale = step_size * lax.rsqrt(squares / (ROWS * n_strip * COLS) + epsilon)
        theta_new = theta_now - d_theta * scale
        if last:
            out_theta[...] = theta_new
            for c in res_copies:
                c.wait_recv()
            for q in range(n_src):
                out_resist[:, q * LANES : (q + 1) * LANES] = res[q]
        else:
            thw[...] = theta_new
    for c in pending:
        c.wait_send()


def per_device_fused(n_src, n_strip, theta, target, source_shift, source_weight):
    tables = [jnp.asarray(t) for t in host_tables()]
    total = n_src * SRC_DEV
    part = KEPT // 2
    vm = pl.BlockSpec(memory_space=pltpu.VMEM)
    sm = pl.BlockSpec(memory_space=pltpu.SMEM)
    f32, bf16, dma = jnp.float32, jnp.bfloat16, pltpu.SemaphoreType.DMA
    shape = jax.ShapeDtypeStruct((ROWS, COLS), f32)
    ns, nz = n_src - 1, n_strip - 1
    return pl.pallas_call(
        functools.partial(kernel, n_src, n_strip),
        out_shape=(shape, shape),
        in_specs=[sm, sm] + [vm] * 8,
        out_specs=(vm, vm),
        scratch_shapes=[
            pltpu.VMEM((WIN, COLS), f32),
            pltpu.VMEM((ROWS, COLS), bf16),
            pltpu.VMEM((HALO, COLS), bf16),
            pltpu.VMEM((HALO, COLS), bf16),
            pltpu.VMEM((n_src, 3, SRC_DEV, LANES), f32),
            pltpu.VMEM((total, KEPT, LANES), bf16),
            pltpu.VMEM((total // 2, 2 * ROWS, 2 * LANES), f32),
            pltpu.VMEM((ITERS, n_src, part, LANES), f32),
            pltpu.VMEM((ITERS, ns, part, LANES), f32),
            pltpu.VMEM((ITERS, 3, n_src, part, LANES), f32),
            pltpu.VMEM((ITERS, n_strip, 8, LANES), f32),
            pltpu.VMEM((n_src, ROWS, LANES), f32),
            dma((ns,)), dma((ns,)),
            dma((4,)), dma((4,)),
            dma((ITERS, ns)), dma((ITERS, ns)),
            dma((ITERS, 2)), dma((ITERS, 2)),
            dma((ITERS, 3, ns)), dma((ITERS, 3, ns)),
            dma((ITERS, nz)), dma((ITERS, nz)),
            dma((ns,)), dma((ns,)),
        ],
        compiler_params=pltpu.CompilerParams(
            collective_id=0, has_side_effects=True, vmem_limit_bytes=48 * 1024 * 1024
        ),
    )(source_shift, source_weight, theta, target, *tables)


def solution(mesh):
    n_src, n_strip = mesh.shape["src"], mesh.shape["strip"]
    if n_src * LANES == COLS and n_strip > 2:
        body = functools.partial(per_device_fused, n_src, n_strip)
    else:
        body = per_device
    return jax.shard_map(
        body,
        mesh=mesh,
        in_specs=(P(("band", "strip"), None), P(("band", "strip"), None), P("src", None), P("src")),
        out_specs=(P(("band", "strip"), None), P(("band", "strip"), None)),
        check_vma=False,
    )
```

```python
import functools
import math

import jax
import jax.numpy as jnp
import ml_dtypes
import numpy as np
from jax import lax
from jax.experimental import pallas as pl
from jax.experimental.pallas import tpu as pltpu
from jax.sharding import PartitionSpec as P

ROWS = 128
COLS = 512
HALO = 64
FREQ = 128
SRC_DEV = 8
ITERS = 2


steepness = 20.0
dose_level = 0.27
step_size = 1.0
epsilon = 1e-06


def extended(cells, sides, width):
    for axis, dim in sides:
        count = lax.axis_size(axis)
        head = lax.slice_in_dim(cells, 0, width, axis=dim)
        tail = lax.slice_in_dim(cells, cells.shape[dim] - width, cells.shape[dim], axis=dim)
        cells = jnp.concatenate(
            [
                lax.ppermute(tail, axis, [(i, (i + 1) % count) for i in range(count)]),
                cells,
                lax.ppermute(head, axis, [((i + 1) % count, i) for i in range(count)]),
            ],
            axis=dim,
        )
    return cells


def shifted(array, axis, by):
    size = lax.axis_size(axis)
    return lax.ppermute(array, axis, [(i, (i + by) % size) for i in range(size)])


def phase_pair(freq_ids, points, period):
    index = freq_ids[:, None] % period * points[None, :] % period
    angle = 2.0 * math.pi / period * index.astype(jnp.float32)
    return (jnp.cos(angle), jnp.sin(angle))


def build_tables():
    freq_ids = jnp.arange(FREQ, dtype=jnp.int32) - FREQ // 2
    win_len = ROWS + 2 * HALO
    row_cos, row_sin = phase_pair(freq_ids, jnp.arange(win_len, dtype=jnp.int32), win_len)
    forward_rows = (jnp.concatenate([row_cos, -row_sin], 0) / win_len).astype(jnp.bfloat16)
    col_cos, col_sin = phase_pair(freq_ids, jnp.arange(COLS, dtype=jnp.int32), COLS)
    real_part = jnp.concatenate([col_cos.T, -col_sin.T], 1) / COLS
    imag_part = jnp.concatenate([col_sin.T, col_cos.T], 1) / COLS
    forward_cols = jnp.stack([real_part, imag_part], 0).astype(jnp.bfloat16)
    inverse_cols = jnp.concatenate(
        [jnp.concatenate([col_cos, col_sin], 1), jnp.concatenate([-col_sin, col_cos], 1)], 0
    ).astype(jnp.bfloat16)
    inner_cos, inner_sin = phase_pair(freq_ids, jnp.arange(ROWS, dtype=jnp.int32) + HALO, win_len)
    inner_cos, inner_sin = (inner_cos.T, inner_sin.T)
    inverse_rows = jnp.stack(
        [jnp.stack([inner_cos, -inner_sin], 1), jnp.stack([inner_sin, inner_cos], 1)], 0
    ).astype(jnp.bfloat16)
    return (forward_rows, forward_cols, inverse_cols, inverse_rows)


def pupil_of(shifts):
    grid = jnp.arange(FREQ, dtype=jnp.int32) - FREQ // 2
    along_k = grid[None, :] + shifts[:, 0:1]
    along_l = grid[None, :] + shifts[:, 1:2]
    radius = FREQ // 4
    inside = (
        along_k[:, :, None] * along_k[:, :, None] + along_l[:, None, :] * along_l[:, None, :]
        <= radius * radius
    )
    pupil = inside.astype(jnp.float32)
    return jnp.concatenate([pupil, pupil], 2).astype(jnp.bfloat16)


def imaging(window, pupil, weights, tables, total_sources):
    forward_rows, forward_cols, inverse_cols, inverse_rows = tables
    count = pupil.shape[0]
    half = jnp.dot(forward_rows, window, preferred_element_type=jnp.float32).astype(jnp.bfloat16)
    spectrum = jnp.einsum(
        "pkc,pcl->kl", half.reshape(2, FREQ, COLS), forward_cols, preferred_element_type=jnp.float32
    ).astype(jnp.bfloat16)
    passed = pupil * spectrum[None]
    columns = jnp.dot(
        passed.reshape(count * FREQ, 2 * FREQ), inverse_cols, preferred_element_type=jnp.float32
    ).astype(jnp.bfloat16)
    columns = columns.reshape(count, FREQ, 2, COLS)
    field = jnp.einsum("pxqk,skqc->spxc", inverse_rows, columns, preferred_element_type=jnp.float32)
    scaled = weights / total_sources
    partial_sum = jnp.sum(scaled[:, None, None, None] * field * field, axis=(0, 1))
    return (field, partial_sum)


def adjoint_spectrum(field, d_int, pupil, weights, tables, total_sources):
    forward_rows, forward_cols, inverse_cols, inverse_rows = tables
    count = pupil.shape[0]
    coeff = 2.0 * weights / total_sources
    d_field = (coeff[:, None, None, None] * d_int[None, None] * field).astype(jnp.bfloat16)
    d_columns = jnp.einsum(
        "pxqk,spxc->skqc", inverse_rows, d_field, preferred_element_type=jnp.float32
    ).astype(jnp.bfloat16)
    d_passed = jnp.dot(
        d_columns.reshape(count * FREQ, 2 * COLS),
        inverse_cols.T,
        preferred_element_type=jnp.float32,
    )
    d_passed = d_passed.reshape(count, FREQ, 2 * FREQ)
    return jnp.sum(d_passed * pupil.astype(jnp.float32), axis=0)


def adjoint_window(d_spectrum, tables):
    forward_rows, forward_cols, inverse_cols, inverse_rows = tables
    d_half = jnp.einsum(
        "kl,pcl->pkc", d_spectrum, forward_cols.astype(jnp.float32), precision=lax.Precision.HIGHEST
    )
    d_half = d_half.reshape(2 * FREQ, COLS)
    return jnp.dot(forward_rows.astype(jnp.float32).T, d_half, precision=lax.Precision.HIGHEST)


def per_device(theta, target, source_shift, source_weight):
    tables = build_tables()
    pupil = pupil_of(source_shift)
    total_sources = SRC_DEV * lax.axis_size("src")
    total_cells = ROWS * lax.axis_size("strip") * COLS
    target_rows = target.astype(jnp.float32)
    resist = jnp.zeros((ROWS, COLS), jnp.float32)
    for iteration in range(ITERS):
        mask_now = jax.nn.sigmoid(theta)
        mask_low = mask_now.astype(jnp.bfloat16)
        window = extended(mask_low, (("strip", 0),), HALO)
        field, partial_sum = imaging(window, pupil, source_weight, tables, total_sources)
        intensity = lax.psum(partial_sum, "src")
        resist = jax.nn.sigmoid(steepness * (intensity - dose_level))
        d_int = 2.0 * (resist - target_rows) * steepness * resist * (1.0 - resist)
        d_spectrum = adjoint_spectrum(field, d_int, pupil, source_weight, tables, total_sources)
        d_window = adjoint_window(lax.psum(d_spectrum, "src"), tables)
        from_next = shifted(d_window[:HALO], "strip", -1)
        from_prev = shifted(d_window[HALO + ROWS :], "strip", 1)
        gradient = d_window[HALO : HALO + ROWS]
        gradient = gradient.at[:HALO].add(from_prev)
        gradient = gradient.at[ROWS - HALO :].add(from_next)
        d_theta = gradient * mask_now * (1.0 - mask_now)
        squares = lax.psum(jnp.sum(d_theta * d_theta), "strip")
        theta = theta - step_size * d_theta * lax.rsqrt(squares / total_cells + epsilon)
    return (theta, resist)


MESH = pl.DeviceIdType.MESH
LANES = 128
FIRST = FREQ // 2 - 3 * FREQ // 8
KEPT = FREQ - FIRST
WIN = ROWS + 2 * HALO
STEP = 8


def host_tables():
    freq = np.arange(FREQ) - FREQ // 2

    def pair(ids, points, period):
        angle = 2.0 * np.pi / period * (ids[:, None] % period * points[None, :] % period)
        return np.cos(angle).astype(np.float32), np.sin(angle).astype(np.float32)

    kept = freq[FIRST:]
    rc, rs = pair(kept, np.arange(WIN), WIN)
    rows = np.concatenate([rc, -rs], 0) / WIN
    cc, cs = pair(freq, np.arange(COLS), COLS)
    gc = np.concatenate([cc, -cs], 0)
    gs = np.concatenate([cs, cc], 0)
    ic, si = pair(kept, np.arange(ROWS) + HALO, WIN)
    inv = np.block([[ic.T, -si.T], [si.T, ic.T]])
    return [a.astype(ml_dtypes.bfloat16) for a in (rows, rows.T.copy(), gc, gs, inv, inv.T.copy())]


def dot(a, b):
    return jnp.dot(a, b, preferred_element_type=jnp.float32)


def dot_t(a, b):
    return lax.dot_general(a, b, (((1,), (1,)), ((), ())), preferred_element_type=jnp.float32)


def split2(a):
    high = a.astype(jnp.bfloat16)
    return high, (a - high.astype(jnp.float32)).astype(jnp.bfloat16)


def kernel(
    n_src, n_strip,
    shift_ref, weight_ref, theta_hbm, target_hbm,
    fr_hbm, frt_hbm, gc_hbm, gs_hbm, inv_hbm, invt_hbm,
    out_theta, out_resist,
    thw, mask_own, mask_top, mask_bot, pk, pupil, field, dsp, rs_in, gath, gbuf, res,
    pk_s, pk_r, halo_s, halo_r, rs_s, rs_r, z_s, z_r, ag_s, ag_r, g_s, g_r, res_s, res_r,
    theta_ref, target_ref, fr_ref, frt_ref, gc_ref, gs_ref, inv_ref, invt_ref, in_s,
):
    me = lax.axis_index("src")
    strip = lax.axis_index("strip")
    total = n_src * SRC_DEV
    src_peers = [lax.rem(me + d, n_src) for d in range(1, n_src)]
    strip_peers = [lax.rem(strip + d, n_strip) for d in range(1, n_strip)]
    nxt, prv = strip_peers[0], strip_peers[-1]

    def send(here, there, ssem, rsem, **to):
        copy = pltpu.make_async_remote_copy(
            src_ref=here, dst_ref=there, send_sem=ssem, recv_sem=rsem, device_id=to, device_id_type=MESH
        )
        copy.start()
        pending.append(copy)
        return copy

    def fetch(here, there):
        copy = pltpu.make_async_copy(here, there, in_s.at[len(fetches)])
        copy.start()
        fetches.append(copy)
        return copy

    pending, fetches = [], []
    theta_in = fetch(theta_hbm, theta_ref)
    fr_in = fetch(fr_hbm, fr_ref)
    gc_in, gs_in = fetch(gc_hbm, gc_ref), fetch(gs_hbm, gs_ref)
    inv_in, target_in = fetch(inv_hbm, inv_ref), fetch(target_hbm, target_ref)
    invt_in, frt_in = fetch(invt_hbm, invt_ref), fetch(frt_hbm, frt_ref)
    barrier = pltpu.get_barrier_semaphore()
    for p in src_peers:
        pl.semaphore_signal(barrier, inc=1, device_id={"src": p}, device_id_type=MESH)
    for p in strip_peers:
        pl.semaphore_signal(barrier, inc=1, device_id={"strip": p}, device_id_type=MESH)

    for i in range(SRC_DEV):
        pk[me, 0, i : i + 1, :] = jnp.full((1, LANES), shift_ref[0, i].astype(jnp.float32))
        pk[me, 1, i : i + 1, :] = jnp.full((1, LANES), shift_ref[1, i].astype(jnp.float32))
        pk[me, 2, i : i + 1, :] = jnp.full((1, LANES), weight_ref[i] / total)
    theta_in.wait()
    mask_own[...] = jax.nn.sigmoid(theta_ref[...]).astype(jnp.bfloat16)
    thw[HALO : HALO + ROWS, :] = theta_ref[...]
    pl.semaphore_wait(barrier, n_src - 1 + n_strip - 1)

    down = send(mask_own.at[ROWS - HALO :], mask_top, halo_s.at[0], halo_r.at[0], strip=nxt)
    up = send(mask_own.at[:HALO], mask_bot, halo_s.at[1], halo_r.at[1], strip=prv)
    packs = [send(pk.at[me], pk.at[me], pk_s.at[d], pk_r.at[d], src=p) for d, p in enumerate(src_peers)]
    th_down = send(theta_ref.at[ROWS - HALO :], thw.at[:HALO], halo_s.at[2], halo_r.at[2], strip=nxt)
    th_up = send(theta_ref.at[:HALO], thw.at[HALO + ROWS :], halo_s.at[3], halo_r.at[3], strip=prv)

    col = pl.ds(pl.multiple_of(me * LANES, LANES), LANES)
    for c in fetches[1:]:
        c.wait()
    g_mine = jnp.concatenate([gc_ref[:, col], gs_ref[:, col]], 1)
    target_mine = target_ref[:, col].astype(jnp.float32)

    for c in packs:
        c.wait_recv()

    k_id = lax.broadcasted_iota(jnp.int32, (KEPT, LANES), 0) + (FIRST - FREQ // 2)
    l_id = lax.broadcasted_iota(jnp.int32, (KEPT, LANES), 1) - FREQ // 2
    k_id, l_id = k_id.astype(jnp.float32), l_id.astype(jnp.float32)
    radius = float((FREQ // 4) ** 2)

    def make_pupil(s, carry):
        q, i = s // SRC_DEV, s % SRC_DEV
        a = k_id + pk[q, 0, pl.ds(i, 1), :]
        b = l_id + pk[q, 1, pl.ds(i, 1), :]
        pupil[s] = jnp.where(a * a + b * b <= radius, 1.0, 0.0).astype(jnp.bfloat16)
        return carry

    lax.fori_loop(0, total, make_pupil, 0)
    down.wait_recv()
    up.wait_recv()

    for it in range(ITERS):
        last = it == ITERS - 1
        if it == 0:
            window = jnp.concatenate([mask_top[...], mask_own[...], mask_bot[...]], 0)
        else:
            window = jax.nn.sigmoid(thw[...]).astype(jnp.bfloat16)
        half = dot(fr_ref[...], window).astype(jnp.bfloat16)
        spectrum = dot_t(half[:KEPT], gc_ref[...]) + dot_t(half[KEPT:], gs_ref[...])
        spectrum = (spectrum / COLS).astype(jnp.bfloat16)

        def forward(step, acc):
            inv = inv_ref[...]
            for pair in range(STEP // 2):
                stacked = []
                for j in range(2):
                    p = pupil[step * STEP + 2 * pair + j]
                    passed = spectrum * jnp.concatenate([p, p], 1)
                    cols = dot(passed, g_mine).astype(jnp.bfloat16)
                    stacked.append(jnp.concatenate([cols[:, :LANES], cols[:, LANES:]], 0))
                f = dot(inv, jnp.concatenate(stacked, 1))
                field[step * (STEP // 2) + pair] = f
                f2 = f * f
                for j in range(2):
                    w = pk[step, 2, 2 * pair + j : 2 * pair + j + 1, :]
                    part = f2[:, j * LANES : (j + 1) * LANES]
                    acc = acc + w * (part[:ROWS] + part[ROWS:])
            return acc

        intensity = lax.fori_loop(0, total // STEP, forward, jnp.zeros((ROWS, LANES), jnp.float32))
        resist = jax.nn.sigmoid(steepness * (intensity - dose_level))
        if last:
            res[me] = resist
            res_copies = [
                send(res.at[me], res.at[me], res_s.at[d], res_r.at[d], src=p)
                for d, p in enumerate(src_peers)
            ]
        d_int = 2.0 * (resist - target_mine) * steepness * resist * (1.0 - resist)

        def backward(step, acc):
            invt = invt_ref[...]
            for pair in range(STEP // 2):
                f = field[step * (STEP // 2) + pair]
                scaled = []
                for j in range(2):
                    w = 2.0 * pk[step, 2, 2 * pair + j : 2 * pair + j + 1, :]
                    d = w * d_int
                    scaled.append(jnp.concatenate([d, d], 0) * f[:, j * LANES : (j + 1) * LANES])
                d_field = jnp.concatenate(scaled, 1).astype(jnp.bfloat16)
                d_cols = dot(invt, d_field).astype(jnp.bfloat16)
                for j in range(2):
                    mine = d_cols[:, j * LANES : (j + 1) * LANES]
                    flat = jnp.concatenate([mine[:KEPT], mine[KEPT:]], 1)
                    p = pupil[step * STEP + 2 * pair + j].astype(jnp.float32)
                    acc = acc + jnp.concatenate([p, p], 1) * dot_t(flat, g_mine)
            return acc

        d_spec = lax.fori_loop(0, total // STEP, backward, jnp.zeros((KEPT, 2 * LANES), jnp.float32))
        part = KEPT // 2
        for q in range(n_src):
            r, c = q // 2, q % 2
            dsp[it, q] = d_spec[r * part : (r + 1) * part, c * LANES : (c + 1) * LANES]
        scatter = [
            send(dsp.at[it, p], rs_in.at[it, d], rs_s.at[it, d], rs_r.at[it, d], src=p)
            for d, p in enumerate(src_peers)
        ]
        mine = dsp[it, me]
        for d, c in enumerate(scatter):
            c.wait_recv()
            mine = mine + rs_in[it, d]
        gath[it, 0, me] = mine
        z_next = send(gath.at[it, 0, me], gath.at[it, 1, me], z_s.at[it, 0], z_r.at[it, 0], strip=nxt)
        z_prev = send(gath.at[it, 0, me], gath.at[it, 2, me], z_s.at[it, 1], z_r.at[it, 1], strip=prv)

        def share(rel):
            return [
                send(gath.at[it, rel, me], gath.at[it, rel, me], ag_s.at[it, rel, d], ag_r.at[it, rel, d], src=p)
                for d, p in enumerate(src_peers)
            ]

        shares = share(0)
        z_next.wait_recv()
        shares = shares + share(1)
        z_prev.wait_recv()
        shares = shares + share(2)

        def d_half(rel):
            full = jnp.concatenate(
                [jnp.concatenate([gath[it, rel, 0], gath[it, rel, 1]], 1),
                 jnp.concatenate([gath[it, rel, 2], gath[it, rel, 3]], 1)], 0)
            high, low = split2(full / COLS)
            both = jnp.concatenate([high, low], 0)
            out = []
            for g in (gc_ref, gs_ref):
                o = dot(both, g[...])
                out.append(o[:KEPT] + o[KEPT:])
            return split2(jnp.concatenate(out, 0))

        def back_rows(lo, hi, parts):
            t = frt_ref[lo:hi, :]
            return dot(t, parts[0]) + dot(t, parts[1])

        for c in shares[: n_src - 1]:
            c.wait_recv()
        own = d_half(0)
        center = back_rows(HALO, HALO + ROWS, own) if last else back_rows(0, WIN, own)
        for c in shares[n_src - 1 : 2 * (n_src - 1)]:
            c.wait_recv()
        prev = d_half(1)
        top = back_rows(HALO + ROWS if last else ROWS, WIN, prev)
        for c in shares[2 * (n_src - 1) :]:
            c.wait_recv()
        after = d_half(2)
        bottom = back_rows(0, HALO if last else WIN - ROWS, after)
        gradient = center + jnp.concatenate([top, bottom], 0)
        if it == 0:
            th_down.wait_recv()
            th_up.wait_recv()
        theta_now = thw[HALO : HALO + ROWS, :] if last else thw[...]
        m = jax.nn.sigmoid(theta_now)
        d_theta = gradient * m * (1.0 - m)
        inner = d_theta if last else d_theta[HALO : HALO + ROWS]
        sq = inner * inner
        sq = jnp.sum(sq.reshape(ROWS // 8, 8, COLS), axis=0)
        tile = sq[:, :LANES]
        for c in range(1, COLS // LANES):
            tile = tile + sq[:, c * LANES : (c + 1) * LANES]
        gbuf[it, strip] = tile
        norms = [
            send(gbuf.at[it, strip], gbuf.at[it, strip], g_s.at[it, d], g_r.at[it, d], strip=p)
            for d, p in enumerate(strip_peers)
        ]
        for c in norms:
            c.wait_recv()
        squares = jnp.sum(gbuf[it], axis=0)
        squares = jnp.sum(jnp.sum(squares, axis=1, keepdims=True), axis=0, keepdims=True)
        scale = step_size * lax.rsqrt(squares / (ROWS * n_strip * COLS) + epsilon)
        theta_new = theta_now - d_theta * scale
        if last:
            out_theta[...] = theta_new
            for c in res_copies:
                c.wait_recv()
            for q in range(n_src):
                out_resist[:, q * LANES : (q + 1) * LANES] = res[q]
        else:
            thw[...] = theta_new
    for c in pending:
        c.wait_send()


def per_device_fused(n_src, n_strip, theta, target, source_shift, source_weight):
    tables = [jnp.asarray(t) for t in host_tables()]
    total = n_src * SRC_DEV
    part = KEPT // 2
    vm = pl.BlockSpec(memory_space=pltpu.VMEM)
    hbm = pl.BlockSpec(memory_space=pltpu.HBM)
    sm = pl.BlockSpec(memory_space=pltpu.SMEM)
    f32, bf16, dma = jnp.float32, jnp.bfloat16, pltpu.SemaphoreType.DMA
    shape = jax.ShapeDtypeStruct((ROWS, COLS), f32)
    ns, nz = n_src - 1, n_strip - 1
    return pl.pallas_call(
        functools.partial(kernel, n_src, n_strip),
        out_shape=(shape, shape),
        in_specs=[sm, sm] + [hbm] * 8,
        out_specs=(vm, vm),
        scratch_shapes=[
            pltpu.VMEM((WIN, COLS), f32),
            pltpu.VMEM((ROWS, COLS), bf16),
            pltpu.VMEM((HALO, COLS), bf16),
            pltpu.VMEM((HALO, COLS), bf16),
            pltpu.VMEM((n_src, 3, SRC_DEV, LANES), f32),
            pltpu.VMEM((total, KEPT, LANES), bf16),
            pltpu.VMEM((total // 2, 2 * ROWS, 2 * LANES), f32),
            pltpu.VMEM((ITERS, n_src, part, LANES), f32),
            pltpu.VMEM((ITERS, ns, part, LANES), f32),
            pltpu.VMEM((ITERS, 3, n_src, part, LANES), f32),
            pltpu.VMEM((ITERS, n_strip, 8, LANES), f32),
            pltpu.VMEM((n_src, ROWS, LANES), f32),
            dma((ns,)), dma((ns,)),
            dma((4,)), dma((4,)),
            dma((ITERS, ns)), dma((ITERS, ns)),
            dma((ITERS, 2)), dma((ITERS, 2)),
            dma((ITERS, 3, ns)), dma((ITERS, 3, ns)),
            dma((ITERS, nz)), dma((ITERS, nz)),
            dma((ns,)), dma((ns,)),
            pltpu.VMEM((ROWS, COLS), f32),
            pltpu.VMEM((ROWS, COLS), jnp.int32),
            *[pltpu.VMEM(t.shape, bf16) for t in tables],
            dma((8,)),
        ],
        compiler_params=pltpu.CompilerParams(
            collective_id=0, has_side_effects=True, vmem_limit_bytes=64 * 1024 * 1024
        ),
    )(source_shift.T, source_weight, theta, target, *tables)


def solution(mesh):
    n_src, n_strip = mesh.shape["src"], mesh.shape["strip"]
    if n_src * LANES == COLS and n_strip > 2:
        body = functools.partial(per_device_fused, n_src, n_strip)
    else:
        body = per_device
    return jax.shard_map(
        body,
        mesh=mesh,
        in_specs=(P(("band", "strip"), None), P(("band", "strip"), None), P("src", None), P("src")),
        out_specs=(P(("band", "strip"), None), P(("band", "strip"), None)),
        check_vma=False,
    )
```
